512 devices in a mesh: row: 16 (over z_hi, y), col: 32 (over x, z_lo, core).
Axes of the slice: x: 4, y: 8, z: 8 (z_hi: 2, z_lo: 4; z = z_hi * 4 + z_lo), core: 2. Of those that a mesh axis runs over, the one named last changes fastest.
Arguments:
- amplitudes: float32 [6, 16, 128, 2048], P(None, None, 'col', 'row'), may hold values from -0.054 to 0.054
- integrals: float32 [12, 16, 128, 2048], P(None, None, 'col', 'row'), may hold values from -6 to 6
- occupied_left: float32 [6], replicated, may hold values from -2 to -0.5
- occupied_right: float32 [12], replicated, may hold values from -2 to -0.5
- virtual_energy: float32 [2048], replicated, may hold values from 0.5 to 3
Outputs:
- update: float32 [6, 12, 16, 128, 2048], P(None, None, None, 'col', 'row')
The draws below stay inside these ranges and needn't reach their ends.
All inputs are finite; a program needn't handle non-finite values.
Results may differ from the reference program's by a relative error of at most 0.00007.
Values sent between devices are 32-bit elements; how exact they have to be, the bound alone decides.
A program may use at most 192 MiB of HBM per device.

```python
import jax
import jax.numpy as jnp
from jax import lax

V = 2048
OI = 6
OJ = 12
NQB = 16
NQ2 = 128


def block_levels(own_key, dims, shards, least, high):
    def one(axis_at, shards_of):
        draws = jax.random.uniform(jax.random.fold_in(jax.random.fold_in(own_key, 6), axis_at), (shards_of,), jnp.float32, least / len(shards), high / len(shards))
        return jnp.repeat(jnp.exp(draws), dims[axis_at] // shards_of).reshape((-1,) + (1,) * (len(dims) - axis_at - 1))

    factor_of = one(*shards[0])
    for cut in shards[1:]:
        factor_of = factor_of * one(*cut)
    return factor_of


def centred(stream_key, shape, width, limit, shards=(), held_as=jnp.bfloat16):
    drawn = width * jax.random.normal(stream_key, shape, jnp.float32)
    if shards:
        drawn = drawn * block_levels(stream_key, shape, shards, -0.22, 0.18)
    return jnp.clip(drawn, -limit, limit).astype(held_as)


def setup_inputs(seed: int = 0) -> dict:
    key_of = jax.random.split(jax.random.key(seed), 6)
    amplitudes = centred(key_of[0], (OI, NQB, NQ2, V), 0.009, 0.054, ((2, 32), (3, 16)), jnp.float32)
    integrals = centred(key_of[1], (OJ, NQB, NQ2, V), 1.0, 6.0, ((2, 32), (3, 16)), jnp.float32)
    occupied_left = jnp.clip(jax.random.uniform(key_of[2], (OI,), jnp.float32, -2.0, -0.5), -2.0, -0.5)
    occupied_right = jnp.clip(jax.random.uniform(key_of[3], (OJ,), jnp.float32, -2.0, -0.5), -2.0, -0.5)
    virtual_energy = jnp.clip(jax.random.uniform(key_of[4], (V,), jnp.float32, 0.5, 3.0), 0.5, 3.0)
    return {"amplitudes": amplitudes, "integrals": integrals, "occupied_left": occupied_left, "occupied_right": occupied_right, "virtual_energy": virtual_energy}


def reference(amplitudes, integrals, occupied_left, occupied_right, virtual_energy):
    stored_amp = amplitudes.reshape(OI, V, V)
    tilde = 2.0 * stored_amp - jnp.swapaxes(stored_amp, 1, 2)
    stored_int = integrals.reshape(OJ, V, V)
    lmat = 2.0 * stored_int - jnp.swapaxes(stored_int, 1, 2)

    def one_orbital(pieces):
        tilde_row, energy_i = pieces
        cycle = jnp.einsum("ca,jbc->jba", tilde_row, lmat, precision=lax.Precision.HIGHEST)
        denom = virtual_energy[None, None, :] + virtual_energy[None, :, None] - energy_i - occupied_right[:, None, None]
        return (cycle / denom).reshape(OJ, NQB, NQ2, V)

    return lax.map(one_orbital, (tilde, occupied_left))
```

```python
import functools
import heapq

import jax
import jax.numpy as jnp
from jax import lax
from jax.experimental import pallas as pl
from jax.experimental.pallas import tpu as pltpu
from jax.sharding import PartitionSpec as P

MESH = pl.DeviceIdType.MESH
LANES = 128
F32 = jnp.float32
BF16 = jnp.bfloat16

ROW_DIMS = (2, 8)
COL_DIMS = (4, 4, 2)
GROUPS = 2


class Links:
    def __init__(self):
        self.free = {}

    def send(self, link, now, size):
        start = max(now, self.free.get(link, 0.0))
        self.free[link] = start + size
        return start + size + 1.0


def split(x):
    high = x.astype(BF16)
    return high, (x - high.astype(F32)).astype(BF16)


def load_tile(ref, b):
    return ref.reshape(-1, LANES, LANES)[b]


def store_tile(ref, b, value):
    ref.reshape(-1, LANES, LANES)[b] = value


def swap_low_digits(x, digit):
    rows = lax.broadcasted_iota(jnp.int32, x.shape, 0)
    lanes = lax.broadcasted_iota(jnp.int32, x.shape, 1)
    bit = 1
    while bit < digit:
        row_bit, lane_bit = rows & bit, lanes & bit
        upper = pltpu.roll(pltpu.roll(x, x.shape[0] - bit, 0), bit, 1)
        lower = pltpu.roll(pltpu.roll(x, bit, 0), x.shape[1] - bit, 1)
        x = jnp.where(row_bit == lane_bit, x, jnp.where(lane_bit == bit, upper, lower))
        bit *= 2
    return x


def kernel(
    left_count,
    right_count,
    int_hbm,
    amp_hbm,
    occ_left,
    occ_right,
    energy,
    out_hbm,
    int_own,
    amp_own,
    int_row,
    amp_row,
    int_send,
    amp_send,
    int_col,
    amp_col,
    lm,
    tl,
    lhs,
    rhs,
    acc,
    recip,
    base,
    staged,
    own_sem,
    keep_sem,
    row_send,
    row_recv,
    col_send,
    col_recv,
    lm_send,
    lm_recv,
    tl_send,
    tl_recv,
    out_sem,
):
    halves, ring = ROW_DIMS
    xs, runs, cores = COL_DIMS
    rows, cols = halves * ring, xs * runs * cores
    sub = LANES // cols
    cells = rows * sub
    r, s = lax.axis_index("row"), lax.axis_index("col")
    half, y = r // ring, r % ring
    x, run, core = s // (runs * cores), (s // cores) % runs, s % cores
    per_group = right_count // GROUPS
    group_rows = per_group * cells
    blocks = group_rows // LANES
    amp_blocks = left_count * cells // LANES

    def row_of(a, b):
        return a * ring + b

    def col_of(a, b, c):
        return (a * runs + b) * cores + c

    def remote(src, dst, send_sem, recv_sem, device):
        return pltpu.make_async_remote_copy(
            src_ref=src,
            dst_ref=dst,
            send_sem=send_sem,
            recv_sem=recv_sem,
            device_id=device,
            device_id_type=MESH,
        )

    own_copies = [
        pltpu.make_async_copy(int_hbm, int_own, own_sem.at[0]),
        pltpu.make_async_copy(amp_hbm, amp_own, own_sem.at[1]),
    ]
    for copy in own_copies:
        copy.start()

    barrier = pltpu.get_barrier_semaphore()

    def greet_row(k, carry):
        pl.semaphore_signal(barrier, inc=1, device_id=((r + k) % rows, s), device_id_type=MESH)
        return carry

    def greet_col(k, carry):
        pl.semaphore_signal(barrier, inc=1, device_id=(r, (s + k) % cols), device_id_type=MESH)
        return carry

    lax.fori_loop(1, rows, greet_row, 0)
    lax.fori_loop(1, cols, greet_col, 0)
    pl.semaphore_wait(barrier, rows - 1 + cols - 1)

    parts = []
    for g in range(GROUPS):
        numbers = pl.ds(g * per_group, per_group)
        slabs = pl.ds(g * blocks, blocks)
        parts.append((int_hbm, int_row, int_send, int_col, numbers, slabs, g * blocks, blocks))
    everything = pl.ds(0, left_count)
    parts.append(
        (amp_hbm, amp_row, amp_send, amp_col, everything, pl.ds(0, amp_blocks), 0, amp_blocks)
    )

    keeps = []
    for n, (source, landed, _, _, numbers, _, _, _) in enumerate(parts):

        def send_row(k, carry, n=n, source=source, landed=landed, numbers=numbers):
            to = (r + k) % rows
            remote(
                source.at[numbers, to],
                landed.at[numbers, r],
                row_send.at[n],
                row_recv.at[n],
                (to, s),
            ).start()
            return carry

        lax.fori_loop(1, rows, send_row, 0)
        keep = pltpu.make_async_copy(source.at[numbers, r], landed.at[numbers, r], keep_sem.at[n])
        keep.start()
        keeps.append(keep)

    own_energy = energy[pl.ds(r, 1), :]
    lane = lax.broadcasted_iota(jnp.int32, (sub, LANES), 1)
    wanted = lax.broadcasted_iota(jnp.int32, (sub, LANES), 0) + sub * s
    for u in range(rows):
        spread = jnp.broadcast_to(energy[u : u + 1, :], (sub, LANES))
        chosen = jnp.sum(jnp.where(lane == wanted, spread, 0.0), axis=1, keepdims=True)
        base[u] = own_energy + chosen
    both_energies = base[...].reshape(cells, LANES)

    def reciprocals(j, carry):
        for i in range(left_count):
            recip[i, j] = 1.0 / (both_energies - occ_left[i] - occ_right[j])
        return carry

    lax.fori_loop(0, right_count, reciprocals, 0)

    def row_part(n):
        source, landed, turned, arrived, numbers, slabs, first, count = parts[n]
        if rows > 1:
            whole = landed.at[numbers, pl.ds(0, rows - 1)]
            both = remote(whole, whole, row_send.at[n], row_recv.at[n], (r, (s + 1) % cols))
            both.wait_recv()
        keeps[n].wait()
        for b in range(first, first + count):
            store_tile(turned, b, load_tile(landed, b).T)

        def send_col(k, carry):
            to = (s + k) % cols
            remote(
                turned.at[slabs, to],
                arrived.at[slabs, s],
                col_send.at[n],
                col_recv.at[n],
                (r, to),
            ).start()
            return carry

        lax.fori_loop(1, cols, send_col, 0)
        for b in range(first, first + count):
            arrived[b, s] = turned[b, s]

    def col_part(n):
        source, landed, turned, arrived, numbers, slabs, first, count = parts[n]
        whole = arrived.at[slabs, pl.ds(0, cols - 1)]
        remote(whole, whole, col_send.at[n], col_recv.at[n], (r, (s + 1) % cols)).wait_recv()
        own, into = (int_own, lm.at[r]) if n < GROUPS else (amp_own, tl.at[s])
        for b in range(first, first + count):
            moved = swap_low_digits(load_tile(arrived, b).T, sub)
            store_tile(into, b, 2.0 * load_tile(own, b) - moved)

    def finish_sends(n):
        source, landed, turned, arrived, numbers, slabs, first, count = parts[n]
        if rows > 1:
            whole = landed.at[numbers, pl.ds(0, rows - 1)]
            remote(whole, whole, row_send.at[n], row_recv.at[n], (r, (s + 1) % cols)).wait_send()
        whole = arrived.at[slabs, pl.ds(0, cols - 1)]
        remote(whole, whole, col_send.at[n], col_recv.at[n], (r, (s + 1) % cols)).wait_send()

    sends = []
    count_of = {"lm": 0, "tl": 0}
    links = Links()
    heap = []
    serial = [0]

    def at(time, act):
        serial[0] += 1
        heapq.heappush(heap, (time, serial[0], act))

    def lm_chunk(slot, g):
        return lm.at[slot, pl.ds(g * group_rows, group_rows)]

    def send_lm(slot, g, device):
        chunk = lm_chunk(slot, g)
        copy = remote(chunk, chunk, lm_send.at[count_of["lm"]], lm_recv.at[slot, g], device)
        count_of["lm"] += 1
        copy.start()
        sends.append(copy)

    def await_lm(slot, g):
        chunk = lm_chunk(slot, g)
        remote(chunk, chunk, lm_send.at[0], lm_recv.at[slot, g], (r, (s + 1) % cols)).wait_recv()

    def send_tl(slot, device):
        chunk = tl.at[slot]
        copy = remote(chunk, chunk, tl_send.at[count_of["tl"]], tl_recv.at[slot], device)
        count_of["tl"] += 1
        copy.start()
        sends.append(copy)

    def await_tl(slot):
        chunk = tl.at[slot]
        remote(chunk, chunk, tl_send.at[0], tl_recv.at[slot], (r, (s + 1) % cols)).wait_recv()

    lm_ready, tl_ready = {}, []
    far_y, far_x = ring // 2, xs // 2
    lm_time = group_rows * LANES * 4 * 2 / 100e3
    tl_time = left_count * cells * LANES * 4 * 2 / 100e3

    def ways(distance, far, parity):
        if distance + 1 < far:
            return (1, -1)
        return ((1,) if parity else (-1,)) if distance + 1 == far else ()

    def spread_lm(now, z, g, distance, came):
        place = half if z == 0 else (half + z) % halves
        slot = row_of(place, (y - came * distance) % ring)
        if distance:
            await_lm(slot, g)
        elif z:
            await_lm(slot, g)
        lm_ready.setdefault(came * distance % ring, []).append(now)
        for way in ways(distance, far_y, (z + g) % 2):
            if distance == 0 or way == came:
                send_lm(slot, g, (row_of(half, (y + way) % ring), s))
                then = links.send(("y", way), now, lm_time)
                at(then, functools.partial(spread_lm, then, z, g, distance + 1, way))
        if z == 0 and distance == 0:
            for k in range(1, halves):
                send_lm(slot, g, (row_of((half + k) % halves, y), s))
                then = links.send("half", now, 2 * lm_time)
                at(then, functools.partial(spread_lm, then, k, g, 0, 1))
        compute(now)

    def spread_tl(now, k, distance, came, first):
        slot = col_of((x - came * distance) % xs, (run - k) % runs, core)
        if not first:
            await_tl(slot)
        tl_ready.append(now)
        for way in ways(distance, far_x, k % 2):
            if distance == 0 or way == came:
                send_tl(slot, (r, col_of((x + way) % xs, run, core)))
                then = links.send(("x", way), now, tl_time)
                at(then, functools.partial(spread_tl, then, k, distance + 1, way, False))
        if first:
            for other in range(1, runs):
                send_tl(slot, (r, col_of(x, (run + other) % runs, core)))
                then = links.send("run", now, tl_time)
                at(then, functools.partial(spread_tl, then, other, 0, 1, False))
        if cores > 1:
            send_tl(slot, (r, col_of(x, run, 1 - core)))
            then = links.send("core", now, tl_time / 6)
            at(then, functools.partial(sibling, then, k, distance, came))
        compute(now)

    def sibling(now, k, distance, came):
        await_tl(col_of((x - came * distance) % xs, (run - k) % runs, 1 - core))
        tl_ready.append(now)
        compute(now)

    def start_lm(now, g):
        col_part(g)
        spread_lm(now, 0, g, 0, 1)

    def start_tl(now):
        col_part(GROUPS)
        spread_tl(now, 0, 0, 1, True)

    done = set()

    def compute(now):
        if len(tl_ready) < cols:
            return
        for place, times in list(lm_ready.items()):
            if len(times) == halves * GROUPS and place not in done:
                products(place, not done)
                done.add(place)

    def products(place, first):
        at_y = (y - place) % ring
        width = halves * LANES
        for z in range(halves):
            slot = row_of(z, at_y)

            def left(b, carry, z=z, slot=slot):
                here = pl.ds(pl.multiple_of(b * LANES, LANES), LANES)
                high, low = split(lm[slot, here, :])
                lhs[here, z * LANES : (z + 1) * LANES] = high
                lhs[here, width + z * LANES : width + (z + 1) * LANES] = low
                lhs[here, 2 * width + z * LANES : 2 * width + (z + 1) * LANES] = high
                return carry

            lax.fori_loop(0, right_count * cells // LANES, left, 0)
            for i in range(left_count):
                high, low = split(tl[:, i, slot].reshape(LANES, LANES))
                across = slice(i * LANES, (i + 1) * LANES)
                rhs[z * LANES : (z + 1) * LANES, across] = high
                rhs[width + z * LANES : width + (z + 1) * LANES, across] = high
                rhs[2 * width + z * LANES : 2 * width + (z + 1) * LANES, across] = low
        tile = 256

        def multiply(m, carry):
            here = pl.ds(pl.multiple_of(m * tile, tile), tile)
            for n in range(left_count * LANES // tile):
                across = slice(n * tile, (n + 1) * tile)
                product = jnp.dot(lhs[here, :], rhs[:, across], preferred_element_type=F32)
                acc[here, across] = product if first else acc[here, across] + product
            return carry

        lax.fori_loop(0, right_count * cells // tile, multiply, 0)

    def turn(n):
        return lambda: row_part(n)

    for n in range(GROUPS + 1):
        at(4.0 + n, turn(n))
    for g in range(GROUPS):
        at(10.0 + 2.0 * g, functools.partial(start_lm, 10.0 + 2.0 * g, g))
    start = 10.0 + 2.0 * GROUPS
    at(start, functools.partial(start_tl, start))
    for copy in own_copies:
        at(9.0, copy.wait)
    while heap:
        heapq.heappop(heap)[2]()
    assert len(done) == ring

    def finish(j, carry):
        here = pl.ds(pl.multiple_of(j * cells, cells), cells)
        for i in range(left_count):
            result = acc[here, i * LANES : (i + 1) * LANES] * recip[i, j]
            staged[i, j] = result.reshape(rows, sub, LANES)
        pltpu.make_async_copy(staged.at[:, j], out_hbm.at[:, j], out_sem.at[j]).start()
        return carry

    lax.fori_loop(0, right_count, finish, 0)
    for n in range(GROUPS + 1):
        finish_sends(n)
    for copy in sends:
        copy.wait_send()

    def written(j, carry):
        pltpu.make_async_copy(staged.at[:, j], out_hbm.at[:, j], out_sem.at[j]).wait()
        return carry

    lax.fori_loop(0, right_count, written, 0)


def body(amplitudes, integrals, occupied_left, occupied_right, virtual_energy):
    left_count, rows, sub, width = amplitudes.shape
    right_count = integrals.shape[0]
    cols = width // sub
    cells = rows * sub
    amp_blocks, int_blocks = left_count * cells // LANES, right_count * cells // LANES
    depth = 3 * ROW_DIMS[0] * LANES
    dma = pltpu.SemaphoreType.DMA
    anywhere = pl.BlockSpec(memory_space=pl.ANY)
    scalars = pl.BlockSpec(memory_space=pltpu.SMEM)
    return pl.pallas_call(
        functools.partial(kernel, left_count, right_count),
        out_shape=jax.ShapeDtypeStruct((left_count, right_count, rows, sub, width), F32),
        in_specs=[
            anywhere,
            anywhere,
            scalars,
            scalars,
            pl.BlockSpec(memory_space=pltpu.VMEM),
        ],
        out_specs=anywhere,
        scratch_shapes=[
            pltpu.VMEM(integrals.shape, F32),
            pltpu.VMEM(amplitudes.shape, F32),
            pltpu.VMEM(integrals.shape, F32),
            pltpu.VMEM(amplitudes.shape, F32),
            pltpu.VMEM((int_blocks, cols, sub, LANES), F32),
            pltpu.VMEM((amp_blocks, cols, sub, LANES), F32),
            pltpu.VMEM((int_blocks, cols, sub, LANES), F32),
            pltpu.VMEM((amp_blocks, cols, sub, LANES), F32),
            pltpu.VMEM((rows, right_count * cells, LANES), F32),
            pltpu.VMEM((cols,) + amplitudes.shape, F32),
            pltpu.VMEM((right_count * cells, depth), BF16),
            pltpu.VMEM((depth, left_count * LANES), BF16),
            pltpu.VMEM((right_count * cells, left_count * LANES), F32),
            pltpu.VMEM((left_count, right_count, cells, LANES), F32),
            pltpu.VMEM((rows, sub, LANES), F32),
            pltpu.VMEM((left_count, right_count, rows, sub, LANES), F32),
            dma((2,)),
            dma((GROUPS + 1,)),
            dma((GROUPS + 1,)),
            dma((GROUPS + 1,)),
            dma((GROUPS + 1,)),
            dma((GROUPS + 1,)),
            dma((16 * GROUPS,)),
            dma((rows, GROUPS)),
            dma((40,)),
            dma((cols,)),
            dma((right_count,)),
        ],
        compiler_params=pltpu.CompilerParams(
            collective_id=0, has_side_effects=True, vmem_limit_bytes=60 * 1024 * 1024
        ),
    )(
        integrals,
        amplitudes,
        occupied_left,
        occupied_right,
        virtual_energy.reshape(rows, width),
    )


def solution(mesh):
    return jax.shard_map(
        body,
        mesh=mesh,
        in_specs=(P(None, None, "col", "row"), P(None, None, "col", "row"), P(), P(), P()),
        out_specs=P(None, None, None, "col", "row"),
        check_vma=False,
    )
```

```python
import functools
import heapq

import jax
import jax.numpy as jnp
from jax import lax
from jax.experimental import pallas as pl
from jax.experimental.pallas import tpu as pltpu
from jax.sharding import PartitionSpec as P

MESH = pl.DeviceIdType.MESH
LANES = 128
F32 = jnp.float32
BF16 = jnp.bfloat16

ROW_DIMS = (2, 8)
COL_DIMS = (4, 4, 2)
GROUPS = 3
AMP_TURN = 1
RING_SENT = (0.0, 0.0, 0.0, 0.0)
RING_DONE = (4.5, 7.0, 9.5, 12.5)
PLANE_DONE = (11.0, 15.0, 18.0, 21.0)
HALF_SENT = (26.0, 26.1, 26.2)
Y_FREE = 12.0
Z_FREE = 14.0


class Links:
    def __init__(self):
        self.free = {}

    def send(self, link, now, size):
        start = max(now, self.free.get(link, 0.0))
        self.free[link] = start + size
        return start + size + 1.0


def split(x):
    high = x.astype(BF16)
    return high, (x - high.astype(F32)).astype(BF16)


def load_tile(ref, b):
    return ref.reshape(-1, LANES, LANES)[b]


def store_tile(ref, b, value):
    ref.reshape(-1, LANES, LANES)[b] = value


def swap_low_digits(x, digit):
    rows = lax.broadcasted_iota(jnp.int32, x.shape, 0)
    lanes = lax.broadcasted_iota(jnp.int32, x.shape, 1)
    bit = 1
    while bit < digit:
        row_bit, lane_bit = rows & bit, lanes & bit
        upper = pltpu.roll(pltpu.roll(x, x.shape[0] - bit, 0), bit, 1)
        lower = pltpu.roll(pltpu.roll(x, bit, 0), x.shape[1] - bit, 1)
        x = jnp.where(row_bit == lane_bit, x, jnp.where(lane_bit == bit, upper, lower))
        bit *= 2
    return x


def kernel(
    left_count,
    right_count,
    int_hbm,
    amp_hbm,
    occ_left,
    occ_right,
    energy,
    out_hbm,
    int_own,
    amp_own,
    int_row,
    amp_row,
    int_send,
    amp_send,
    int_col,
    amp_col,
    lm,
    tl,
    lhs,
    rhs,
    acc,
    recip,
    base,
    staged,
    own_sem,
    keep_sem,
    ring_send,
    ring_recv,
    plane_send,
    plane_recv,
    lm_send,
    lm_recv,
    tl_send,
    tl_recv,
    out_sem,
):
    halves, ring = ROW_DIMS
    xs, runs, cores = COL_DIMS
    rows, cols = halves * ring, xs * runs * cores
    sub = LANES // cols
    cells = rows * sub
    r, s = lax.axis_index("row"), lax.axis_index("col")
    half, y = r // ring, r % ring
    x, run, core = s // (runs * cores), (s // cores) % runs, s % cores
    per_group = right_count // GROUPS
    group_rows = per_group * cells
    stretch = ring * sub
    per_tile = LANES // stretch
    tiles = per_group // per_tile
    amp_tiles = pl.cdiv(left_count, per_tile)

    def row_of(a, b):
        return a * ring + b

    def col_of(a, b, c):
        return (a * runs + b) * cores + c

    plane = halves * cols
    me = half * cols + s

    def in_plane(number):
        return row_of(number // cols, y), number % cols

    def remote(src, dst, send_sem, recv_sem, device):
        return pltpu.make_async_remote_copy(
            src_ref=src,
            dst_ref=dst,
            send_sem=send_sem,
            recv_sem=recv_sem,
            device_id=device,
            device_id_type=MESH,
        )

    own_copies = [
        pltpu.make_async_copy(int_hbm, int_own, own_sem.at[0]),
        pltpu.make_async_copy(amp_hbm, amp_own, own_sem.at[1]),
    ]
    for copy in own_copies:
        copy.start()

    barrier = pltpu.get_barrier_semaphore()

    def greet_ring(k, carry):
        to = row_of(half, (y + k) % ring)
        pl.semaphore_signal(barrier, inc=1, device_id=(to, s), device_id_type=MESH)
        return carry

    def greet_plane(k, carry):
        pl.semaphore_signal(barrier, inc=1, device_id=in_plane((me + k) % plane), device_id_type=MESH)
        return carry

    lax.fori_loop(1, ring, greet_ring, 0)
    lax.fori_loop(1, plane, greet_plane, 0)
    pl.semaphore_wait(barrier, ring - 1 + plane - 1)

    parts = []
    for g in range(GROUPS):
        numbers = pl.ds(g * per_group, per_group)
        parts.append((int_hbm, int_row, int_send, int_col, numbers, range(g * tiles, (g + 1) * tiles)))
    parts.append((amp_hbm, amp_row, amp_send, amp_col, pl.ds(0, left_count), range(amp_tiles)))
    for h in range(halves):
        for i in range(left_count, amp_tiles * per_tile):
            amp_row[h, i] = jnp.zeros((ring, sub, LANES), F32)

    order = list(range(GROUPS))
    order.insert(AMP_TURN, GROUPS)
    keeps = {}

    def start_ring(n):
        source, landed, _, _, numbers, _ = parts[n]

        def send_ring(k, carry):
            to = (y + k) % ring
            for h in range(halves):
                remote(
                    source.at[numbers, h, to],
                    landed.at[h, numbers, y],
                    ring_send.at[n],
                    ring_recv.at[n],
                    (row_of(half, to), s),
                ).start()
            return carry

        lax.fori_loop(1, ring, send_ring, 0)
        keeps[n] = []
        for h in range(halves):
            keep = pltpu.make_async_copy(
                source.at[numbers, h, y], landed.at[h, numbers, y], keep_sem.at[n, h]
            )
            keep.start()
            keeps[n].append(keep)

    for k, n in enumerate(order):
        if RING_SENT[k] == 0:
            start_ring(n)

    own_energy = energy[pl.ds(r, 1), :]
    lane = lax.broadcasted_iota(jnp.int32, (sub, LANES), 1)
    wanted = lax.broadcasted_iota(jnp.int32, (sub, LANES), 0) + sub * s
    for u in range(rows):
        spread = jnp.broadcast_to(energy[u : u + 1, :], (sub, LANES))
        chosen = jnp.sum(jnp.where(lane == wanted, spread, 0.0), axis=1, keepdims=True)
        base[u] = own_energy + chosen
    both_energies = base[...].reshape(cells, LANES)

    def reciprocals(j, carry):
        for i in range(left_count):
            recip[i, j] = 1.0 / (both_energies - occ_left[i] - occ_right[j])
        return carry

    lax.fori_loop(0, right_count, reciprocals, 0)

    def ring_wait(n):
        _, landed, _, _, numbers, _ = parts[n]
        whole = landed.at[:, numbers, pl.ds(0, ring - 1)]
        return remote(whole, whole, ring_send.at[n], ring_recv.at[n], (r, (s + 1) % cols))

    def plane_wait(n):
        _, _, _, arrived, _, numbers = parts[n]
        whole = arrived.at[pl.ds(numbers.start, len(numbers)), pl.ds(0, plane - 1)]
        return remote(whole, whole, plane_send.at[n], plane_recv.at[n], (r, (s + 1) % cols))

    def ring_part(n):
        _, landed, turned, arrived, _, numbers = parts[n]
        if ring > 1:
            ring_wait(n).wait_recv()
        for keep in keeps[n]:
            keep.wait()
        count = landed.shape[1] // per_tile
        for k in numbers:
            for h in range(halves):
                store_tile(turned, k * halves + h, load_tile(landed, h * count + k).T)
        slabs = pl.ds(numbers.start, len(numbers))

        def send_plane(k, carry):
            to = (me + k) % plane
            remote(
                turned.at[slabs, to],
                arrived.at[slabs, me],
                plane_send.at[n],
                plane_recv.at[n],
                in_plane(to),
            ).start()
            return carry

        lax.fori_loop(1, plane, send_plane, 0)
        for k in numbers:
            arrived[k, me] = turned[k, me]

    def plane_part(n):
        _, _, _, arrived, _, numbers = parts[n]
        plane_wait(n).wait_recv()
        for k in numbers:
            for h in range(halves):
                moved = swap_low_digits(load_tile(arrived, k * halves + h).T, sub)
                for part in range(per_tile):
                    number = k * per_tile + part
                    piece = moved[part * stretch : (part + 1) * stretch]
                    if n < GROUPS:
                        own = int_own[number, h].reshape(stretch, LANES)
                        first = number * cells + h * stretch
                        lm[r, first : first + stretch, :] = 2.0 * own - piece
                    elif number < left_count:
                        own = amp_own[number, h]
                        into = slice(h * ring, (h + 1) * ring)
                        tl[s, number, into] = 2.0 * own - piece.reshape(own.shape)

    def finish_sends(n):
        if ring > 1:
            ring_wait(n).wait_send()
        plane_wait(n).wait_send()

    sends = []
    count_of = {"lm": 0, "tl": 0}
    links = Links()
    links.free = {("y", 1): Y_FREE, ("y", -1): Y_FREE, "z": Z_FREE}
    heap = []
    serial = [0]

    def at(time, act):
        serial[0] += 1
        heapq.heappush(heap, (time, serial[0], act))

    def lm_chunk(slot, g):
        return lm.at[slot, pl.ds(g * group_rows, group_rows)]

    def send_lm(slot, g, device):
        chunk = lm_chunk(slot, g)
        copy = remote(chunk, chunk, lm_send.at[count_of["lm"]], lm_recv.at[slot, g], device)
        count_of["lm"] += 1
        copy.start()
        sends.append(copy)

    def await_lm(slot, g):
        chunk = lm_chunk(slot, g)
        remote(chunk, chunk, lm_send.at[0], lm_recv.at[slot, g], (r, (s + 1) % cols)).wait_recv()

    def send_tl(slot, device):
        chunk = tl.at[slot]
        copy = remote(chunk, chunk, tl_send.at[count_of["tl"]], tl_recv.at[slot], device)
        count_of["tl"] += 1
        copy.start()
        sends.append(copy)

    def await_tl(slot):
        chunk = tl.at[slot]
        remote(chunk, chunk, tl_send.at[0], tl_recv.at[slot], (r, (s + 1) % cols)).wait_recv()

    lm_ready, tl_ready = {}, []
    far_y, far_x = ring // 2, xs // 2
    lm_time = group_rows * LANES * 4 * 2 / 100e3
    tl_time = left_count * cells * LANES * 4 * 2 / 100e3

    def ways(distance, far, parity):
        if distance + 1 < far:
            return (1, -1)
        return ((1,) if parity else (-1,)) if distance + 1 == far else ()

    def spread_lm(now, z, g, distance, came):
        place = half if z == 0 else (half + z) % halves
        slot = row_of(place, (y - came * distance) % ring)
        if distance:
            await_lm(slot, g)
        elif z:
            await_lm(slot, g)
        lm_ready.setdefault((came * distance % ring, g), []).append(now)
        for way in ways(distance, far_y, (z + g) % 2):
            if distance == 0 or way == came:
                send_lm(slot, g, (row_of(half, (y + way) % ring), s))
                then = links.send(("y", way), now, lm_time)
                at(then, functools.partial(spread_lm, then, z, g, distance + 1, way))
        if z == 0 and distance == 0:
            later = max(now, HALF_SENT[g])
            at(later, functools.partial(cross, later, g))
        compute(now)

    def cross(now, g):
        for k in range(1, halves):
            send_lm(row_of(half, y), g, (row_of((half + k) % halves, y), s))
            then = links.send("z", now, 2 * lm_time)
            at(then, functools.partial(spread_lm, then, k, g, 0, 1))

    def spread_tl(now, k, distance, came, first):
        slot = col_of((x - came * distance) % xs, (run - k) % runs, core)
        if not first:
            await_tl(slot)
        tl_ready.append(now)
        for way in ways(distance, far_x, k % 2):
            if distance == 0 or way == came:
                send_tl(slot, (r, col_of((x + way) % xs, run, core)))
                then = links.send(("x", way), now, tl_time)
                at(then, functools.partial(spread_tl, then, k, distance + 1, way, False))
        if first:
            for other in range(1, runs):
                send_tl(slot, (r, col_of(x, (run + other) % runs, core)))
                then = links.send("z", now, tl_time)
                at(then, functools.partial(spread_tl, then, other, 0, 1, False))
        if cores > 1:
            send_tl(slot, (r, col_of(x, run, 1 - core)))
            then = links.send("core", now, tl_time / 6)
            at(then, functools.partial(sibling, then, k, distance, came))
        compute(now)

    def sibling(now, k, distance, came):
        await_tl(col_of((x - came * distance) % xs, (run - k) % runs, 1 - core))
        tl_ready.append(now)
        compute(now)

    def start_lm(now, g):
        plane_part(g)
        spread_lm(now, 0, g, 0, 1)

    def start_tl(now):
        plane_part(GROUPS)
        spread_tl(now, 0, 0, 1, True)

    prepared, done, finished = set(), set(), set()
    waiting = []

    def compute(now):
        if len(tl_ready) < cols:
            return
        if not waiting:
            waiting.append(now)
            for n, place in enumerate(nearest):
                at(now + 0.7 * n, functools.partial(prepare, now + 0.7 * n, place))
        for place in nearest:
            for g in range(GROUPS):
                ready = len(lm_ready.get((place, g), ())) == halves and place in prepared
                if ready and (place, g) not in done:
                    products(place, g, not any(other == g for _, other in done))
                    done.add((place, g))
        for g in range(GROUPS):
            if g not in finished and sum(other == g for _, other in done) == ring:
                finish(g)
                finished.add(g)

    nearest = sorted(range(ring), key=lambda place: min(place, ring - place))
    width = halves * LANES

    def prepare(now, place):
        at_y = (y - place) % ring

        def right(k, carry):
            z = k // left_count
            i = k % left_count
            high, low = split(tl[:, i, z * ring + at_y].reshape(LANES, LANES))
            across = pl.ds(pl.multiple_of(i * LANES, LANES), LANES)
            here = pl.multiple_of(z * LANES, LANES)
            rhs[at_y, pl.ds(here, LANES), across] = high
            rhs[at_y, pl.ds(width + here, LANES), across] = high
            rhs[at_y, pl.ds(2 * width + here, LANES), across] = low
            return carry

        lax.fori_loop(0, halves * left_count, right, 0)
        prepared.add(place)
        compute(now)

    def products(place, g, first):
        at_y = (y - place) % ring
        for z in range(halves):
            high, low = split(lm[row_of(z, at_y), pl.ds(g * group_rows, group_rows), :])
            lhs[:, z * LANES : (z + 1) * LANES] = high
            lhs[:, width + z * LANES : width + (z + 1) * LANES] = low
            lhs[:, 2 * width + z * LANES : 2 * width + (z + 1) * LANES] = high
        tile = 256
        here = pl.ds(g * group_rows, group_rows)

        def multiply(n, carry):
            across = pl.ds(pl.multiple_of(n * tile, tile), tile)
            product = jnp.dot(lhs[...], rhs[at_y, :, across], preferred_element_type=F32)
            acc[here, across] = product if first else acc[here, across] + product
            return carry

        lax.fori_loop(0, left_count * LANES // tile, multiply, 0)

    def finish(g):
        def scale(k, carry):
            j = g * per_group + k
            here = pl.ds(pl.multiple_of(j * cells, cells), cells)
            for i in range(left_count):
                result = acc[here, i * LANES : (i + 1) * LANES] * recip[i, j]
                staged[i, j] = result.reshape(rows, sub, LANES)
            pltpu.make_async_copy(staged.at[:, j], out_hbm.at[:, j], out_sem.at[j]).start()
            return carry

        lax.fori_loop(0, per_group, scale, 0)

    def turn(n):
        return lambda: ring_part(n)

    for k, n in enumerate(order):
        if RING_SENT[k] > 0:
            at(RING_SENT[k] + 0.01, functools.partial(start_ring, n))
        at(RING_DONE[k], turn(n))
        began = PLANE_DONE[k]
        if n < GROUPS:
            at(began, functools.partial(start_lm, began, n))
        else:
            at(began, functools.partial(start_tl, began))
    for copy in own_copies:
        at(min(PLANE_DONE) - 0.5, copy.wait)
    while heap:
        heapq.heappop(heap)[2]()
    assert len(finished) == GROUPS

    for n in range(GROUPS + 1):
        finish_sends(n)
    for copy in sends:
        copy.wait_send()

    def written(j, carry):
        pltpu.make_async_copy(staged.at[:, j], out_hbm.at[:, j], out_sem.at[j]).wait()
        return carry

    lax.fori_loop(0, right_count, written, 0)


def body(amplitudes, integrals, occupied_left, occupied_right, virtual_energy):
    left_count, rows, sub, width = amplitudes.shape
    right_count = integrals.shape[0]
    cols = width // sub
    cells = rows * sub
    halves, ring = ROW_DIMS
    per_tile = LANES // (ring * sub)
    int_tiles, amp_tiles = right_count // per_tile, pl.cdiv(left_count, per_tile)
    depth = 3 * halves * LANES
    plane = halves * cols
    dma = pltpu.SemaphoreType.DMA
    anywhere = pl.BlockSpec(memory_space=pl.ANY)
    scalars = pl.BlockSpec(memory_space=pltpu.SMEM)
    return pl.pallas_call(
        functools.partial(kernel, left_count, right_count),
        out_shape=jax.ShapeDtypeStruct((left_count, right_count, rows, sub, width), F32),
        in_specs=[
            anywhere,
            anywhere,
            scalars,
            scalars,
            pl.BlockSpec(memory_space=pltpu.VMEM),
        ],
        out_specs=anywhere,
        scratch_shapes=[
            pltpu.VMEM((right_count, halves, ring, sub, LANES), F32),
            pltpu.VMEM((left_count, halves, ring, sub, LANES), F32),
            pltpu.VMEM((halves, right_count, ring, sub, LANES), F32),
            pltpu.VMEM((halves, amp_tiles * per_tile, ring, sub, LANES), F32),
            pltpu.VMEM((int_tiles, plane, sub, LANES), F32),
            pltpu.VMEM((amp_tiles, plane, sub, LANES), F32),
            pltpu.VMEM((int_tiles, plane, sub, LANES), F32),
            pltpu.VMEM((amp_tiles, plane, sub, LANES), F32),
            pltpu.VMEM((rows, right_count * cells, LANES), F32),
            pltpu.VMEM((cols,) + amplitudes.shape, F32),
            pltpu.VMEM((right_count // GROUPS * cells, depth), BF16),
            pltpu.VMEM((ROW_DIMS[1], depth, left_count * LANES), BF16),
            pltpu.VMEM((right_count * cells, left_count * LANES), F32),
            pltpu.VMEM((left_count, right_count, cells, LANES), F32),
            pltpu.VMEM((rows, sub, LANES), F32),
            pltpu.VMEM((left_count, right_count, rows, sub, LANES), F32),
            dma((2,)),
            dma((GROUPS + 1, halves)),
            dma((GROUPS + 1,)),
            dma((GROUPS + 1,)),
            dma((GROUPS + 1,)),
            dma((GROUPS + 1,)),
            dma((16 * GROUPS,)),
            dma((rows, GROUPS)),
            dma((40,)),
            dma((cols,)),
            dma((right_count,)),
        ],
        compiler_params=pltpu.CompilerParams(
            collective_id=0, has_side_effects=True, vmem_limit_bytes=60 * 1024 * 1024
        ),
    )(
        integrals.reshape(right_count, halves, ring, sub, width),
        amplitudes.reshape(left_count, halves, ring, sub, width),
        occupied_left,
        occupied_right,
        virtual_energy.reshape(rows, width),
    )


def solution(mesh):
    return jax.shard_map(
        body,
        mesh=mesh,
        in_specs=(P(None, None, "col", "row"), P(None, None, "col", "row"), P(), P(), P()),
        out_specs=P(None, None, None, "col", "row"),
        check_vma=False,
    )
```

```python
import functools
import heapq

import jax
import jax.numpy as jnp
from jax import lax
from jax.experimental import pallas as pl
from jax.experimental.pallas import tpu as pltpu
from jax.sharding import PartitionSpec as P

MESH = pl.DeviceIdType.MESH
LANES = 128
F32 = jnp.float32
BF16 = jnp.bfloat16

ROW_DIMS = (2, 8)
COL_DIMS = (4, 4, 2)
GROUPS = 3
AMP_TURN = 1
RING_SENT = (0.0, 0.0, 0.0, 0.0)
RING_DONE = (4.5, 7.0, 9.5, 12.5)
PLANE_DONE = (11.0, 15.0, 18.0, 21.0)
HALF_SENT = (0.0, 0.0, 0.0)
RUN_SENT = (26.5, 26.5, 26.5)
Y_FREE = 12.0
Z_FREE = 14.0


class Links:
    def __init__(self):
        self.free = {}

    def send(self, link, now, size):
        start = max(now, self.free.get(link, 0.0))
        self.free[link] = start + size
        return start + size + 1.0


def split(x):
    high = x.astype(BF16)
    return high, (x - high.astype(F32)).astype(BF16)


def load_tile(ref, b):
    return ref.reshape(-1, LANES, LANES)[b]


def store_tile(ref, b, value):
    ref.reshape(-1, LANES, LANES)[b] = value


def swap_low_digits(x, digit):
    rows = lax.broadcasted_iota(jnp.int32, x.shape, 0)
    lanes = lax.broadcasted_iota(jnp.int32, x.shape, 1)
    bit = 1
    while bit < digit:
        row_bit, lane_bit = rows & bit, lanes & bit
        upper = pltpu.roll(pltpu.roll(x, x.shape[0] - bit, 0), bit, 1)
        lower = pltpu.roll(pltpu.roll(x, bit, 0), x.shape[1] - bit, 1)
        x = jnp.where(row_bit == lane_bit, x, jnp.where(lane_bit == bit, upper, lower))
        bit *= 2
    return x


def kernel(
    left_count,
    right_count,
    int_hbm,
    amp_hbm,
    occ_left,
    occ_right,
    energy,
    out_hbm,
    int_own,
    amp_own,
    int_row,
    amp_row,
    int_send,
    amp_send,
    int_col,
    amp_col,
    lm,
    tl,
    lhs,
    rhs,
    acc,
    recip,
    base,
    staged,
    own_sem,
    keep_sem,
    ring_send,
    ring_recv,
    plane_send,
    plane_recv,
    lm_send,
    lm_recv,
    tl_send,
    tl_recv,
    out_sem,
):
    halves, ring = ROW_DIMS
    xs, runs, cores = COL_DIMS
    rows, cols = halves * ring, xs * runs * cores
    sub = LANES // cols
    cells = rows * sub
    r, s = lax.axis_index("row"), lax.axis_index("col")
    half, y = r // ring, r % ring
    x, run, core = s // (runs * cores), (s // cores) % runs, s % cores
    per_group = right_count // GROUPS
    group_rows = per_group * cells
    stretch = ring * sub
    per_tile = LANES // stretch
    tiles = per_group // per_tile
    amp_tiles = pl.cdiv(left_count, per_tile)

    def row_of(a, b):
        return a * ring + b

    def col_of(a, b, c):
        return (a * runs + b) * cores + c

    plane = halves * cols
    me = half * cols + s

    def in_plane(number):
        return row_of(number // cols, y), number % cols

    def remote(src, dst, send_sem, recv_sem, device):
        return pltpu.make_async_remote_copy(
            src_ref=src,
            dst_ref=dst,
            send_sem=send_sem,
            recv_sem=recv_sem,
            device_id=device,
            device_id_type=MESH,
        )

    own_copies = [
        pltpu.make_async_copy(int_hbm, int_own, own_sem.at[0]),
        pltpu.make_async_copy(amp_hbm, amp_own, own_sem.at[1]),
    ]
    for copy in own_copies:
        copy.start()

    barrier = pltpu.get_barrier_semaphore()

    def greet_ring(k, carry):
        to = row_of(half, (y + k) % ring)
        pl.semaphore_signal(barrier, inc=1, device_id=(to, s), device_id_type=MESH)
        return carry

    def greet_plane(k, carry):
        pl.semaphore_signal(barrier, inc=1, device_id=in_plane((me + k) % plane), device_id_type=MESH)
        return carry

    lax.fori_loop(1, ring, greet_ring, 0)
    lax.fori_loop(1, plane, greet_plane, 0)
    pl.semaphore_wait(barrier, ring - 1 + plane - 1)

    parts = []
    for g in range(GROUPS):
        numbers = pl.ds(g * per_group, per_group)
        parts.append((int_hbm, int_row, int_send, int_col, numbers, range(g * tiles, (g + 1) * tiles)))
    parts.append((amp_hbm, amp_row, amp_send, amp_col, pl.ds(0, left_count), range(amp_tiles)))
    for h in range(halves):
        for i in range(left_count, amp_tiles * per_tile):
            amp_row[h, i] = jnp.zeros((ring, sub, LANES), F32)

    order = list(range(GROUPS))
    order.insert(AMP_TURN, GROUPS)
    keeps = {}

    def start_ring(n):
        source, landed, _, _, numbers, _ = parts[n]

        def send_ring(k, carry):
            to = (y + k) % ring
            for h in range(halves):
                remote(
                    source.at[numbers, h, to],
                    landed.at[h, numbers, y],
                    ring_send.at[n],
                    ring_recv.at[n],
                    (row_of(half, to), s),
                ).start()
            return carry

        lax.fori_loop(1, ring, send_ring, 0)
        keeps[n] = []
        for h in range(halves):
            keep = pltpu.make_async_copy(
                source.at[numbers, h, y], landed.at[h, numbers, y], keep_sem.at[n, h]
            )
            keep.start()
            keeps[n].append(keep)

    for k, n in enumerate(order):
        if RING_SENT[k] == 0:
            start_ring(n)

    own_energy = energy[pl.ds(r, 1), :]
    lane = lax.broadcasted_iota(jnp.int32, (sub, LANES), 1)
    wanted = lax.broadcasted_iota(jnp.int32, (sub, LANES), 0) + sub * s
    for u in range(rows):
        spread = jnp.broadcast_to(energy[u : u + 1, :], (sub, LANES))
        chosen = jnp.sum(jnp.where(lane == wanted, spread, 0.0), axis=1, keepdims=True)
        base[u] = own_energy + chosen
    both_energies = base[...].reshape(cells, LANES)

    def reciprocals(j, carry):
        for i in range(left_count):
            recip[i, j] = 1.0 / (both_energies - occ_left[i] - occ_right[j])
        return carry

    lax.fori_loop(0, right_count, reciprocals, 0)

    def ring_wait(n):
        _, landed, _, _, numbers, _ = parts[n]
        whole = landed.at[:, numbers, pl.ds(0, ring - 1)]
        return remote(whole, whole, ring_send.at[n], ring_recv.at[n], (r, (s + 1) % cols))

    def plane_wait(n):
        _, _, _, arrived, _, numbers = parts[n]
        whole = arrived.at[pl.ds(numbers.start, len(numbers)), pl.ds(0, plane - 1)]
        return remote(whole, whole, plane_send.at[n], plane_recv.at[n], (r, (s + 1) % cols))

    def ring_part(n):
        _, landed, turned, arrived, _, numbers = parts[n]
        if ring > 1:
            ring_wait(n).wait_recv()
        for keep in keeps[n]:
            keep.wait()
        count = landed.shape[1] // per_tile
        for k in numbers:
            for h in range(halves):
                store_tile(turned, k * halves + h, load_tile(landed, h * count + k).T)
        slabs = pl.ds(numbers.start, len(numbers))

        def send_plane(k, carry):
            to = (me + k) % plane
            remote(
                turned.at[slabs, to],
                arrived.at[slabs, me],
                plane_send.at[n],
                plane_recv.at[n],
                in_plane(to),
            ).start()
            return carry

        lax.fori_loop(1, plane, send_plane, 0)
        for k in numbers:
            arrived[k, me] = turned[k, me]

    def plane_part(n):
        _, _, _, arrived, _, numbers = parts[n]
        plane_wait(n).wait_recv()
        for k in numbers:
            for h in range(halves):
                moved = swap_low_digits(load_tile(arrived, k * halves + h).T, sub)
                for part in range(per_tile):
                    number = k * per_tile + part
                    piece = moved[part * stretch : (part + 1) * stretch]
                    if n < GROUPS:
                        own = int_own[number, h].reshape(stretch, LANES)
                        first = number * cells + h * stretch
                        lm[r, first : first + stretch, :] = 2.0 * own - piece
                    elif number < left_count:
                        own = amp_own[number, h]
                        into = slice(h * ring, (h + 1) * ring)
                        tl[s, number, into] = 2.0 * own - piece.reshape(own.shape)

    def finish_sends(n):
        if ring > 1:
            ring_wait(n).wait_send()
        plane_wait(n).wait_send()

    sends = []
    count_of = {"lm": 0, "tl": 0}
    links = Links()
    links.free = {("y", 1): Y_FREE, ("y", -1): Y_FREE, "z": Z_FREE}
    heap = []
    serial = [0]

    def at(time, act):
        serial[0] += 1
        heapq.heappush(heap, (time, serial[0], act))

    def lm_chunk(slot, g):
        return lm.at[slot, pl.ds(g * group_rows, group_rows)]

    def send_lm(slot, g, device):
        chunk = lm_chunk(slot, g)
        copy = remote(chunk, chunk, lm_send.at[count_of["lm"]], lm_recv.at[slot, g], device)
        count_of["lm"] += 1
        copy.start()
        sends.append(copy)

    def await_lm(slot, g):
        chunk = lm_chunk(slot, g)
        remote(chunk, chunk, lm_send.at[0], lm_recv.at[slot, g], (r, (s + 1) % cols)).wait_recv()

    def send_tl(slot, device):
        chunk = tl.at[slot]
        copy = remote(chunk, chunk, tl_send.at[count_of["tl"]], tl_recv.at[slot], device)
        count_of["tl"] += 1
        copy.start()
        sends.append(copy)

    def await_tl(slot):
        chunk = tl.at[slot]
        remote(chunk, chunk, tl_send.at[0], tl_recv.at[slot], (r, (s + 1) % cols)).wait_recv()

    lm_ready, tl_ready = {}, []
    far_y, far_x = ring // 2, xs // 2
    lm_time = group_rows * LANES * 4 * 2 / 100e3
    tl_time = left_count * cells * LANES * 4 * 2 / 100e3

    def ways(distance, far, parity):
        if distance + 1 < far:
            return (1, -1)
        return ((1,) if parity else (-1,)) if distance + 1 == far else ()

    def spread_lm(now, z, g, distance, came):
        place = half if z == 0 else (half + z) % halves
        slot = row_of(place, (y - came * distance) % ring)
        if distance:
            await_lm(slot, g)
        elif z:
            await_lm(slot, g)
        lm_ready.setdefault((came * distance % ring, g), []).append(now)
        for way in ways(distance, far_y, (z + g) % 2):
            if distance == 0 or way == came:
                send_lm(slot, g, (row_of(half, (y + way) % ring), s))
                then = links.send(("y", way), now, lm_time)
                at(then, functools.partial(spread_lm, then, z, g, distance + 1, way))
        if z == 0 and distance == 0:
            later = max(now, HALF_SENT[g])
            at(later, functools.partial(cross, later, g))
        compute(now)

    def cross(now, g):
        for k in range(1, halves):
            send_lm(row_of(half, y), g, (row_of((half + k) % halves, y), s))
            then = links.send("z", now, 2 * lm_time)
            at(then, functools.partial(spread_lm, then, k, g, 0, 1))

    def spread_tl(now, k, distance, came, first):
        slot = col_of((x - came * distance) % xs, (run - k) % runs, core)
        if not first:
            await_tl(slot)
        tl_ready.append(now)
        for way in ways(distance, far_x, k % 2):
            if distance == 0 or way == came:
                send_tl(slot, (r, col_of((x + way) % xs, run, core)))
                then = links.send(("x", way), now, tl_time)
                at(then, functools.partial(spread_tl, then, k, distance + 1, way, False))
        if first:
            for other in range(1, runs):
                later = max(now, RUN_SENT[other - 1])
                at(later, functools.partial(along, later, other))
        if cores > 1:
            send_tl(slot, (r, col_of(x, run, 1 - core)))
            then = links.send("core", now, tl_time / 6)
            at(then, functools.partial(sibling, then, k, distance, came))
        compute(now)

    def along(now, other):
        send_tl(col_of(x, run, core), (r, col_of(x, (run + other) % runs, core)))
        then = links.send("z", now, tl_time)
        at(then, functools.partial(spread_tl, then, other, 0, 1, False))

    def sibling(now, k, distance, came):
        await_tl(col_of((x - came * distance) % xs, (run - k) % runs, 1 - core))
        tl_ready.append(now)
        compute(now)

    def start_lm(now, g):
        plane_part(g)
        spread_lm(now, 0, g, 0, 1)

    def start_tl(now):
        plane_part(GROUPS)
        spread_tl(now, 0, 0, 1, True)

    prepared, done, finished = set(), set(), set()
    waiting = []

    def compute(now):
        if len(tl_ready) < cols:
            return
        if not waiting:
            waiting.append(now)
            for n, place in enumerate(nearest):
                at(now + 0.7 * n, functools.partial(prepare, now + 0.7 * n, place))
        for place in nearest:
            for g in range(GROUPS):
                ready = len(lm_ready.get((place, g), ())) == halves and place in prepared
                if ready and (place, g) not in done:
                    products(place, g, not any(other == g for _, other in done))
                    done.add((place, g))
        for g in range(GROUPS):
            if g not in finished and sum(other == g for _, other in done) == ring:
                finish(g)
                finished.add(g)

    nearest = sorted(range(ring), key=lambda place: min(place, ring - place))
    width = halves * LANES

    def prepare(now, place):
        at_y = (y - place) % ring

        def right(k, carry):
            z = k // left_count
            i = k % left_count
            high, low = split(tl[:, i, z * ring + at_y].reshape(LANES, LANES))
            across = pl.ds(pl.multiple_of(i * LANES, LANES), LANES)
            here = pl.multiple_of(z * LANES, LANES)
            rhs[at_y, pl.ds(here, LANES), across] = high
            rhs[at_y, pl.ds(width + here, LANES), across] = high
            rhs[at_y, pl.ds(2 * width + here, LANES), across] = low
            return carry

        lax.fori_loop(0, halves * left_count, right, 0)
        prepared.add(place)
        compute(now)

    def products(place, g, first):
        at_y = (y - place) % ring
        for z in range(halves):
            high, low = split(lm[row_of(z, at_y), pl.ds(g * group_rows, group_rows), :])
            lhs[:, z * LANES : (z + 1) * LANES] = high
            lhs[:, width + z * LANES : width + (z + 1) * LANES] = low
            lhs[:, 2 * width + z * LANES : 2 * width + (z + 1) * LANES] = high
        tile = 256
        here = pl.ds(g * group_rows, group_rows)

        def multiply(n, carry):
            across = pl.ds(pl.multiple_of(n * tile, tile), tile)
            product = jnp.dot(lhs[...], rhs[at_y, :, across], preferred_element_type=F32)
            acc[here, across] = product if first else acc[here, across] + product
            return carry

        lax.fori_loop(0, left_count * LANES // tile, multiply, 0)

    def finish(g):
        def scale(k, carry):
            j = g * per_group + k
            here = pl.ds(pl.multiple_of(j * cells, cells), cells)
            for i in range(left_count):
                result = acc[here, i * LANES : (i + 1) * LANES] * recip[i, j]
                staged[i, j] = result.reshape(rows, sub, LANES)
            pltpu.make_async_copy(staged.at[:, j], out_hbm.at[:, j], out_sem.at[j]).start()
            return carry

        lax.fori_loop(0, per_group, scale, 0)

    def turn(n):
        return lambda: ring_part(n)

    for k, n in enumerate(order):
        if RING_SENT[k] > 0:
            at(RING_SENT[k] + 0.01, functools.partial(start_ring, n))
        at(RING_DONE[k], turn(n))
        began = PLANE_DONE[k]
        if n < GROUPS:
            at(began, functools.partial(start_lm, began, n))
        else:
            at(began, functools.partial(start_tl, began))
    for copy in own_copies:
        at(min(PLANE_DONE) - 0.5, copy.wait)
    while heap:
        heapq.heappop(heap)[2]()
    assert len(finished) == GROUPS

    for n in range(GROUPS + 1):
        finish_sends(n)
    for copy in sends:
        copy.wait_send()

    def written(j, carry):
        pltpu.make_async_copy(staged.at[:, j], out_hbm.at[:, j], out_sem.at[j]).wait()
        return carry

    lax.fori_loop(0, right_count, written, 0)


def body(amplitudes, integrals, occupied_left, occupied_right, virtual_energy):
    left_count, rows, sub, width = amplitudes.shape
    right_count = integrals.shape[0]
    cols = width // sub
    cells = rows * sub
    halves, ring = ROW_DIMS
    per_tile = LANES // (ring * sub)
    int_tiles, amp_tiles = right_count // per_tile, pl.cdiv(left_count, per_tile)
    depth = 3 * halves * LANES
    plane = halves * cols
    dma = pltpu.SemaphoreType.DMA
    anywhere = pl.BlockSpec(memory_space=pl.ANY)
    scalars = pl.BlockSpec(memory_space=pltpu.SMEM)
    return pl.pallas_call(
        functools.partial(kernel, left_count, right_count),
        out_shape=jax.ShapeDtypeStruct((left_count, right_count, rows, sub, width), F32),
        in_specs=[
            anywhere,
            anywhere,
            scalars,
            scalars,
            pl.BlockSpec(memory_space=pltpu.VMEM),
        ],
        out_specs=anywhere,
        scratch_shapes=[
            pltpu.VMEM((right_count, halves, ring, sub, LANES), F32),
            pltpu.VMEM((left_count, halves, ring, sub, LANES), F32),
            pltpu.VMEM((halves, right_count, ring, sub, LANES), F32),
            pltpu.VMEM((halves, amp_tiles * per_tile, ring, sub, LANES), F32),
            pltpu.VMEM((int_tiles, plane, sub, LANES), F32),
            pltpu.VMEM((amp_tiles, plane, sub, LANES), F32),
            pltpu.VMEM((int_tiles, plane, sub, LANES), F32),
            pltpu.VMEM((amp_tiles, plane, sub, LANES), F32),
            pltpu.VMEM((rows, right_count * cells, LANES), F32),
            pltpu.VMEM((cols,) + amplitudes.shape, F32),
            pltpu.VMEM((right_count // GROUPS * cells, depth), BF16),
            pltpu.VMEM((ROW_DIMS[1], depth, left_count * LANES), BF16),
            pltpu.VMEM((right_count * cells, left_count * LANES), F32),
            pltpu.VMEM((left_count, right_count, cells, LANES), F32),
            pltpu.VMEM((rows, sub, LANES), F32),
            pltpu.VMEM((left_count, right_count, rows, sub, LANES), F32),
            dma((2,)),
            dma((GROUPS + 1, halves)),
            dma((GROUPS + 1,)),
            dma((GROUPS + 1,)),
            dma((GROUPS + 1,)),
            dma((GROUPS + 1,)),
            dma((16 * GROUPS,)),
            dma((rows, GROUPS)),
            dma((40,)),
            dma((cols,)),
            dma((right_count,)),
        ],
        compiler_params=pltpu.CompilerParams(
            collective_id=0, has_side_effects=True, vmem_limit_bytes=60 * 1024 * 1024
        ),
    )(
        integrals.reshape(right_count, halves, ring, sub, width),
        amplitudes.reshape(left_count, halves, ring, sub, width),
        occupied_left,
        occupied_right,
        virtual_energy.reshape(rows, width),
    )


def solution(mesh):
    return jax.shard_map(
        body,
        mesh=mesh,
        in_specs=(P(None, None, "col", "row"), P(None, None, "col", "row"), P(), P(), P()),
        out_specs=P(None, None, None, "col", "row"),
        check_vma=False,
    )
```

```python
import functools
import heapq

import jax
import jax.numpy as jnp
from jax import lax
from jax.experimental import pallas as pl
from jax.experimental.pallas import tpu as pltpu
from jax.sharding import PartitionSpec as P

MESH = pl.DeviceIdType.MESH
LANES = 128
F32 = jnp.float32
BF16 = jnp.bfloat16

ROW_DIMS = (2, 8)
COL_DIMS = (4, 4, 2)
GROUPS = 3
AMP_TURN = 1
RING_SENT = (0.0, 0.0, 0.0, 0.0)
RING_DONE = (4.5, 7.0, 9.5, 12.5)
PLANE_DONE = (11.0, 15.0, 18.0, 21.0)
HALF_SENT = (0.0, 0.0, 0.0)
RUN_SENT = (0.0, 26.5, 26.5)
Y_FREE = 12.0
Z_FREE = 14.0


class Links:
    def __init__(self):
        self.free = {}

    def send(self, link, now, size):
        start = max(now, self.free.get(link, 0.0))
        self.free[link] = start + size
        return start + size + 1.0


def split(x):
    high = x.astype(BF16)
    return high, (x - high.astype(F32)).astype(BF16)


def load_tile(ref, b):
    return ref.reshape(-1, LANES, LANES)[b]


def store_tile(ref, b, value):
    ref.reshape(-1, LANES, LANES)[b] = value


def swap_low_digits(x, digit):
    rows = lax.broadcasted_iota(jnp.int32, x.shape, 0)
    lanes = lax.broadcasted_iota(jnp.int32, x.shape, 1)
    bit = 1
    while bit < digit:
        row_bit, lane_bit = rows & bit, lanes & bit
        upper = pltpu.roll(pltpu.roll(x, x.shape[0] - bit, 0), bit, 1)
        lower = pltpu.roll(pltpu.roll(x, bit, 0), x.shape[1] - bit, 1)
        x = jnp.where(row_bit == lane_bit, x, jnp.where(lane_bit == bit, upper, lower))
        bit *= 2
    return x


def kernel(
    left_count,
    right_count,
    int_hbm,
    amp_hbm,
    occ_left,
    occ_right,
    energy,
    out_hbm,
    int_own,
    amp_own,
    int_row,
    amp_row,
    int_send,
    amp_send,
    int_col,
    amp_col,
    lm,
    tl,
    lhs,
    rhs,
    acc,
    recip,
    base,
    staged,
    own_sem,
    keep_sem,
    ring_send,
    ring_recv,
    plane_send,
    plane_recv,
    lm_send,
    lm_recv,
    tl_send,
    tl_recv,
    out_sem,
):
    halves, ring = ROW_DIMS
    xs, runs, cores = COL_DIMS
    rows, cols = halves * ring, xs * runs * cores
    sub = LANES // cols
    cells = rows * sub
    r, s = lax.axis_index("row"), lax.axis_index("col")
    half, y = r // ring, r % ring
    x, run, core = s // (runs * cores), (s // cores) % runs, s % cores
    per_group = right_count // GROUPS
    group_rows = per_group * cells
    stretch = ring * sub
    per_tile = LANES // stretch
    tiles = per_group // per_tile
    amp_tiles = pl.cdiv(left_count, per_tile)

    def row_of(a, b):
        return a * ring + b

    def col_of(a, b, c):
        return (a * runs + b) * cores + c

    plane = halves * cols
    me = half * cols + s

    def in_plane(number):
        return row_of(number // cols, y), number % cols

    def remote(src, dst, send_sem, recv_sem, device):
        return pltpu.make_async_remote_copy(
            src_ref=src,
            dst_ref=dst,
            send_sem=send_sem,
            recv_sem=recv_sem,
            device_id=device,
            device_id_type=MESH,
        )

    own_copies = [
        pltpu.make_async_copy(int_hbm, int_own, own_sem.at[0]),
        pltpu.make_async_copy(amp_hbm, amp_own, own_sem.at[1]),
    ]
    for copy in own_copies:
        copy.start()

    barrier = pltpu.get_barrier_semaphore()

    def greet_ring(k, carry):
        to = row_of(half, (y + k) % ring)
        pl.semaphore_signal(barrier, inc=1, device_id=(to, s), device_id_type=MESH)
        return carry

    def greet_plane(k, carry):
        pl.semaphore_signal(barrier, inc=1, device_id=in_plane((me + k) % plane), device_id_type=MESH)
        return carry

    lax.fori_loop(1, ring, greet_ring, 0)
    lax.fori_loop(1, plane, greet_plane, 0)
    pl.semaphore_wait(barrier, ring - 1 + plane - 1)

    parts = []
    for g in range(GROUPS):
        numbers = pl.ds(g * per_group, per_group)
        parts.append((int_hbm, int_row, int_send, int_col, numbers, range(g * tiles, (g + 1) * tiles)))
    parts.append((amp_hbm, amp_row, amp_send, amp_col, pl.ds(0, left_count), range(amp_tiles)))
    for h in range(halves):
        for i in range(left_count, amp_tiles * per_tile):
            amp_row[h, i] = jnp.zeros((ring, sub, LANES), F32)

    order = list(range(GROUPS))
    order.insert(AMP_TURN, GROUPS)
    keeps = {}

    def start_ring(n):
        source, landed, _, _, numbers, _ = parts[n]

        def send_ring(k, carry):
            to = (y + k) % ring
            for h in range(halves):
                remote(
                    source.at[numbers, h, to],
                    landed.at[h, numbers, y],
                    ring_send.at[n],
                    ring_recv.at[n],
                    (row_of(half, to), s),
                ).start()
            return carry

        lax.fori_loop(1, ring, send_ring, 0)
        keeps[n] = []
        for h in range(halves):
            keep = pltpu.make_async_copy(
                source.at[numbers, h, y], landed.at[h, numbers, y], keep_sem.at[n, h]
            )
            keep.start()
            keeps[n].append(keep)

    for k, n in enumerate(order):
        if RING_SENT[k] == 0:
            start_ring(n)

    own_energy = energy[pl.ds(r, 1), :]
    lane = lax.broadcasted_iota(jnp.int32, (sub, LANES), 1)
    wanted = lax.broadcasted_iota(jnp.int32, (sub, LANES), 0) + sub * s
    for u in range(rows):
        spread = jnp.broadcast_to(energy[u : u + 1, :], (sub, LANES))
        chosen = jnp.sum(jnp.where(lane == wanted, spread, 0.0), axis=1, keepdims=True)
        base[u] = own_energy + chosen
    both_energies = base[...].reshape(cells, LANES)

    def reciprocals(j, carry):
        for i in range(left_count):
            recip[i, j] = 1.0 / (both_energies - occ_left[i] - occ_right[j])
        return carry

    lax.fori_loop(0, right_count, reciprocals, 0)

    def ring_wait(n):
        _, landed, _, _, numbers, _ = parts[n]
        whole = landed.at[:, numbers, pl.ds(0, ring - 1)]
        return remote(whole, whole, ring_send.at[n], ring_recv.at[n], (r, (s + 1) % cols))

    def plane_wait(n):
        _, _, _, arrived, _, numbers = parts[n]
        whole = arrived.at[pl.ds(numbers.start, len(numbers)), pl.ds(0, plane - 1)]
        return remote(whole, whole, plane_send.at[n], plane_recv.at[n], (r, (s + 1) % cols))

    def ring_part(n):
        _, landed, turned, arrived, _, numbers = parts[n]
        if ring > 1:
            ring_wait(n).wait_recv()
        for keep in keeps[n]:
            keep.wait()
        count = landed.shape[1] // per_tile
        for k in numbers:
            for h in range(halves):
                store_tile(turned, k * halves + h, load_tile(landed, h * count + k).T)
        slabs = pl.ds(numbers.start, len(numbers))

        def send_plane(k, carry):
            to = (me + k) % plane
            remote(
                turned.at[slabs, to],
                arrived.at[slabs, me],
                plane_send.at[n],
                plane_recv.at[n],
                in_plane(to),
            ).start()
            return carry

        lax.fori_loop(1, plane, send_plane, 0)
        for k in numbers:
            arrived[k, me] = turned[k, me]

    def plane_part(n):
        _, _, _, arrived, _, numbers = parts[n]
        plane_wait(n).wait_recv()
        for k in numbers:
            for h in range(halves):
                moved = swap_low_digits(load_tile(arrived, k * halves + h).T, sub)
                for part in range(per_tile):
                    number = k * per_tile + part
                    piece = moved[part * stretch : (part + 1) * stretch]
                    if n < GROUPS:
                        own = int_own[number, h].reshape(stretch, LANES)
                        first = number * cells + h * stretch
                        lm[r, first : first + stretch, :] = 2.0 * own - piece
                    elif number < left_count:
                        own = amp_own[number, h]
                        into = slice(h * ring, (h + 1) * ring)
                        tl[s, number, into] = 2.0 * own - piece.reshape(own.shape)

    def finish_sends(n):
        if ring > 1:
            ring_wait(n).wait_send()
        plane_wait(n).wait_send()

    sends = []
    count_of = {"lm": 0, "tl": 0}
    links = Links()
    links.free = {("y", 1): Y_FREE, ("y", -1): Y_FREE, "z": Z_FREE}
    heap = []
    serial = [0]

    def at(time, act):
        serial[0] += 1
        heapq.heappush(heap, (time, serial[0], act))

    def lm_chunk(slot, g):
        return lm.at[slot, pl.ds(g * group_rows, group_rows)]

    def send_lm(slot, g, device):
        chunk = lm_chunk(slot, g)
        copy = remote(chunk, chunk, lm_send.at[count_of["lm"]], lm_recv.at[slot, g], device)
        count_of["lm"] += 1
        copy.start()
        sends.append(copy)

    def await_lm(slot, g):
        chunk = lm_chunk(slot, g)
        remote(chunk, chunk, lm_send.at[0], lm_recv.at[slot, g], (r, (s + 1) % cols)).wait_recv()

    def send_tl(slot, device):
        chunk = tl.at[slot]
        copy = remote(chunk, chunk, tl_send.at[count_of["tl"]], tl_recv.at[slot], device)
        count_of["tl"] += 1
        copy.start()
        sends.append(copy)

    def await_tl(slot):
        chunk = tl.at[slot]
        remote(chunk, chunk, tl_send.at[0], tl_recv.at[slot], (r, (s + 1) % cols)).wait_recv()

    lm_ready, tl_ready = {}, []
    far_y, far_x = ring // 2, xs // 2
    lm_time = group_rows * LANES * 4 * 2 / 100e3
    tl_time = left_count * cells * LANES * 4 * 2 / 100e3

    def ways(distance, far, parity):
        if distance + 1 < far:
            return (1, -1)
        return ((1,) if parity else (-1,)) if distance + 1 == far else ()

    def spread_lm(now, z, g, distance, came):
        place = half if z == 0 else (half + z) % halves
        slot = row_of(place, (y - came * distance) % ring)
        if distance:
            await_lm(slot, g)
        elif z:
            await_lm(slot, g)
        lm_ready.setdefault((came * distance % ring, g), []).append(now)
        for way in ways(distance, far_y, (z + g) % 2):
            if distance == 0 or way == came:
                send_lm(slot, g, (row_of(half, (y + way) % ring), s))
                then = links.send(("y", way), now, lm_time)
                at(then, functools.partial(spread_lm, then, z, g, distance + 1, way))
        if z == 0 and distance == 0:
            later = max(now, HALF_SENT[g])
            at(later, functools.partial(cross, later, g))
        compute(now)

    def cross(now, g):
        for k in range(1, halves):
            send_lm(row_of(half, y), g, (row_of((half + k) % halves, y), s))
            then = links.send("z", now, 2 * lm_time)
            at(then, functools.partial(spread_lm, then, k, g, 0, 1))

    def spread_tl(now, k, distance, came, first):
        slot = col_of((x - came * distance) % xs, (run - k) % runs, core)
        if not first:
            await_tl(slot)
        tl_ready.append(now)
        for way in ways(distance, far_x, k % 2):
            if distance == 0 or way == came:
                send_tl(slot, (r, col_of((x + way) % xs, run, core)))
                then = links.send(("x", way), now, tl_time)
                at(then, functools.partial(spread_tl, then, k, distance + 1, way, False))
        if first:
            for other in range(1, runs):
                later = max(now, RUN_SENT[other - 1])
                at(later, functools.partial(along, later, other))
        if cores > 1:
            send_tl(slot, (r, col_of(x, run, 1 - core)))
            then = links.send("core", now, tl_time / 6)
            at(then, functools.partial(sibling, then, k, distance, came))
        compute(now)

    def along(now, other):
        send_tl(col_of(x, run, core), (r, col_of(x, (run + other) % runs, core)))
        then = links.send("z", now, tl_time)
        at(then, functools.partial(spread_tl, then, other, 0, 1, False))

    def sibling(now, k, distance, came):
        await_tl(col_of((x - came * distance) % xs, (run - k) % runs, 1 - core))
        tl_ready.append(now)
        compute(now)

    def start_lm(now, g):
        plane_part(g)
        spread_lm(now, 0, g, 0, 1)

    def start_tl(now):
        plane_part(GROUPS)
        spread_tl(now, 0, 0, 1, True)

    prepared, done, finished = set(), set(), set()
    waiting = []

    def compute(now):
        if len(tl_ready) < cols:
            return
        if not waiting:
            waiting.append(now)
            for n, place in enumerate(nearest):
                at(now + 0.7 * n, functools.partial(prepare, now + 0.7 * n, place))
        for place in nearest:
            for g in range(GROUPS):
                ready = len(lm_ready.get((place, g), ())) == halves and place in prepared
                if ready and (place, g) not in done:
                    products(place, g, not any(other == g for _, other in done))
                    done.add((place, g))
        for g in range(GROUPS):
            if g not in finished and sum(other == g for _, other in done) == ring:
                finish(g)
                finished.add(g)

    nearest = sorted(range(ring), key=lambda place: min(place, ring - place))
    width = halves * LANES

    def prepare(now, place):
        at_y = (y - place) % ring

        def right(k, carry):
            z = k // left_count
            i = k % left_count
            high, low = split(tl[:, i, z * ring + at_y].reshape(LANES, LANES))
            across = pl.ds(pl.multiple_of(i * LANES, LANES), LANES)
            here = pl.multiple_of(z * LANES, LANES)
            rhs[at_y, pl.ds(here, LANES), across] = high
            rhs[at_y, pl.ds(width + here, LANES), across] = high
            rhs[at_y, pl.ds(2 * width + here, LANES), across] = low
            return carry

        lax.fori_loop(0, halves * left_count, right, 0)
        prepared.add(place)
        compute(now)

    def products(place, g, first):
        at_y = (y - place) % ring
        for z in range(halves):
            high, low = split(lm[row_of(z, at_y), pl.ds(g * group_rows, group_rows), :])
            lhs[:, z * LANES : (z + 1) * LANES] = high
            lhs[:, width + z * LANES : width + (z + 1) * LANES] = low
            lhs[:, 2 * width + z * LANES : 2 * width + (z + 1) * LANES] = high
        tile = 256
        here = pl.ds(g * group_rows, group_rows)

        def multiply(n, carry):
            across = pl.ds(pl.multiple_of(n * tile, tile), tile)
            product = jnp.dot(lhs[...], rhs[at_y, :, across], preferred_element_type=F32)
            acc[here, across] = product if first else acc[here, across] + product
            return carry

        lax.fori_loop(0, left_count * LANES // tile, multiply, 0)

    def finish(g):
        def scale(k, carry):
            j = g * per_group + k
            here = pl.ds(pl.multiple_of(j * cells, cells), cells)
            for i in range(left_count):
                result = acc[here, i * LANES : (i + 1) * LANES] * recip[i, j]
                staged[i, j] = result.reshape(rows, sub, LANES)
            pltpu.make_async_copy(staged.at[:, j], out_hbm.at[:, j], out_sem.at[j]).start()
            return carry

        lax.fori_loop(0, per_group, scale, 0)

    def turn(n):
        return lambda: ring_part(n)

    for k, n in enumerate(order):
        if RING_SENT[k] > 0:
            at(RING_SENT[k] + 0.01, functools.partial(start_ring, n))
        at(RING_DONE[k], turn(n))
        began = PLANE_DONE[k]
        if n < GROUPS:
            at(began, functools.partial(start_lm, began, n))
        else:
            at(began, functools.partial(start_tl, began))
    for copy in own_copies:
        at(min(PLANE_DONE) - 0.5, copy.wait)
    while heap:
        heapq.heappop(heap)[2]()
    assert len(finished) == GROUPS

    for n in range(GROUPS + 1):
        finish_sends(n)
    for copy in sends:
        copy.wait_send()

    def written(j, carry):
        pltpu.make_async_copy(staged.at[:, j], out_hbm.at[:, j], out_sem.at[j]).wait()
        return carry

    lax.fori_loop(0, right_count, written, 0)


def body(amplitudes, integrals, occupied_left, occupied_right, virtual_energy):
    left_count, rows, sub, width = amplitudes.shape
    right_count = integrals.shape[0]
    cols = width // sub
    cells = rows * sub
    halves, ring = ROW_DIMS
    per_tile = LANES // (ring * sub)
    int_tiles, amp_tiles = right_count // per_tile, pl.cdiv(left_count, per_tile)
    depth = 3 * halves * LANES
    plane = halves * cols
    dma = pltpu.SemaphoreType.DMA
    anywhere = pl.BlockSpec(memory_space=pl.ANY)
    scalars = pl.BlockSpec(memory_space=pltpu.SMEM)
    return pl.pallas_call(
        functools.partial(kernel, left_count, right_count),
        out_shape=jax.ShapeDtypeStruct((left_count, right_count, rows, sub, width), F32),
        in_specs=[
            anywhere,
            anywhere,
            scalars,
            scalars,
            pl.BlockSpec(memory_space=pltpu.VMEM),
        ],
        out_specs=anywhere,
        scratch_shapes=[
            pltpu.VMEM((right_count, halves, ring, sub, LANES), F32),
            pltpu.VMEM((left_count, halves, ring, sub, LANES), F32),
            pltpu.VMEM((halves, right_count, ring, sub, LANES), F32),
            pltpu.VMEM((halves, amp_tiles * per_tile, ring, sub, LANES), F32),
            pltpu.VMEM((int_tiles, plane, sub, LANES), F32),
            pltpu.VMEM((amp_tiles, plane, sub, LANES), F32),
            pltpu.VMEM((int_tiles, plane, sub, LANES), F32),
            pltpu.VMEM((amp_tiles, plane, sub, LANES), F32),
            pltpu.VMEM((rows, right_count * cells, LANES), F32),
            pltpu.VMEM((cols,) + amplitudes.shape, F32),
            pltpu.VMEM((right_count // GROUPS * cells, depth), BF16),
            pltpu.VMEM((ROW_DIMS[1], depth, left_count * LANES), BF16),
            pltpu.VMEM((right_count * cells, left_count * LANES), F32),
            pltpu.VMEM((left_count, right_count, cells, LANES), F32),
            pltpu.VMEM((rows, sub, LANES), F32),
            pltpu.VMEM((left_count, right_count, rows, sub, LANES), F32),
            dma((2,)),
            dma((GROUPS + 1, halves)),
            dma((GROUPS + 1,)),
            dma((GROUPS + 1,)),
            dma((GROUPS + 1,)),
            dma((GROUPS + 1,)),
            dma((16 * GROUPS,)),
            dma((rows, GROUPS)),
            dma((40,)),
            dma((cols,)),
            dma((right_count,)),
        ],
        compiler_params=pltpu.CompilerParams(
            collective_id=0, has_side_effects=True, vmem_limit_bytes=60 * 1024 * 1024
        ),
    )(
        integrals.reshape(right_count, halves, ring, sub, width),
        amplitudes.reshape(left_count, halves, ring, sub, width),
        occupied_left,
        occupied_right,
        virtual_energy.reshape(rows, width),
    )


def solution(mesh):
    return jax.shard_map(
        body,
        mesh=mesh,
        in_specs=(P(None, None, "col", "row"), P(None, None, "col", "row"), P(), P(), P()),
        out_specs=P(None, None, None, "col", "row"),
        check_vma=False,
    )
```
